128 devices in a mesh: replica: 4 (over z_lo, core), fsdp: 32 (over x, y, z_hi).
Axes of the slice: x: 4, y: 4, z: 4 (z_hi: 2, z_lo: 2; z = z_hi * 2 + z_lo), core: 2. Of those that a mesh axis runs over, the one named last changes fastest.
Arguments:
- levels: int32 [4, 8192, 8192], P('replica', 'fsdp'), may hold values from -8 to 7
- scales: float32 [4, 8192, 64], P('replica', 'fsdp'), may hold values from 0.02 to 0.2
- master: float32 [8192, 8192], P('replica', 'fsdp'), may hold values from -6 to 6
- momentum: float32 [8192, 8192], P('replica', 'fsdp'), may hold values from -4 to 4
Outputs:
- new_master: float32 [8192, 8192], P('replica', 'fsdp')
- new_momentum: float32 [8192, 8192], P('replica', 'fsdp')
- weights: bfloat16 [8192, 8192], P('fsdp')
The draws below stay inside these ranges and needn't reach their ends.
All inputs are finite; a program needn't handle non-finite values.
Results may differ from the reference program's by a relative error of at most 0.007.
Values may be sent and summed in bfloat16 or wider, within the bound.
A program may use at most 128 MiB of HBM per device.

```python
import math
import jax
import jax.numpy as jnp

D = 8192
BLOCK = 128
REPL = 4


def with_ends(entries, rng, smallest, high):
    place = [jax.random.randint(jax.random.fold_in(rng, axis), (), 0, length) for axis, length in enumerate(entries.shape)]
    longest = entries.shape.index(max(entries.shape))
    neighbour = place[:longest] + [(place[longest] + 1) % entries.shape[longest]] + place[longest + 1:]
    return entries.at[tuple(place)].set(smallest).at[tuple(neighbour)].set(high)


def level_of(rng, extent, pieces, low, top_value):
    loudness, own = 1.0, jax.random.fold_in(rng, 6)
    for axis_at, shards_of in pieces:
        heights = jnp.exp(jax.random.uniform(jax.random.fold_in(own, axis_at), (shards_of,), jnp.float32, low / len(pieces), top_value / len(pieces)))
        loudness = loudness * jnp.repeat(heights, extent[axis_at] // shards_of).reshape([-1 if axis == axis_at else 1 for axis in range(len(extent))])
    return loudness


def gaussian(key, dims, deviation, bound, pieces=(), held_as=jnp.bfloat16):
    drawn = deviation * jax.random.normal(key, dims, jnp.float32)
    if pieces:
        drawn = drawn * level_of(key, dims, pieces, -0.22, 0.18)
    return jnp.clip(drawn, -bound, bound).astype(held_as)


def setup_inputs(seed: int = 0) -> dict:
    key_list = jax.random.split(jax.random.key(seed), 5)
    return {
        "levels": with_ends(jax.random.randint(key_list[0], (REPL, D, D), -8, 8), jax.random.fold_in(key_list[0], 1), -8, 7).astype(jnp.int32),
        "scales": jnp.clip(jnp.exp(math.log(0.2) - 2.3025851 * jax.random.uniform(key_list[1], (REPL, D, D // BLOCK), jnp.float32) ** level_of(key_list[1], (REPL, D, D // BLOCK), ((0, 4), (1, 32)), -0.2, 0.2)), 0.02, 0.2),
        "master": gaussian(key_list[2], (D, D), 1.0, 6.0, ((0, 4), (1, 32)), jnp.float32),
        "momentum": gaussian(key_list[3], (D, D), 0.3, 4.0, ((0, 4), (1, 32)), jnp.float32),
    }


outer_rate = 0.7
momentum_coef = 0.9


def reference(levels, scales, master, momentum):
    summed = jnp.zeros((D, D), jnp.float32)
    for replica in range(REPL):
        blocks = levels[replica].astype(jnp.float32).reshape(D, D // BLOCK, BLOCK)
        decoded = (blocks * scales[replica][:, :, None]).reshape(D, D).astype(jnp.bfloat16)
        summed = summed + decoded.astype(jnp.float32)
    outer_grad = summed / REPL
    new_momentum = momentum_coef * momentum + outer_grad
    new_master = master - outer_rate * (outer_grad + momentum_coef * new_momentum)
    return new_master, new_momentum, new_master.astype(jnp.bfloat16)
```

```python
import functools

import jax
import jax.numpy as jnp
from jax import lax
from jax.experimental import pallas as pl
from jax.experimental.pallas import tpu as pltpu
from jax.sharding import PartitionSpec as P

MESH = pl.DeviceIdType.MESH
F32 = jnp.float32
BF16 = jnp.bfloat16

BLOCK = 128
ROWS = 128
COLS = 256
CHUNKS = 16
LOADS = 8

outer_rate = 0.7
momentum_coef = 0.9
MOM = outer_rate * momentum_coef * momentum_coef
GRAD = outer_rate * (1.0 + momentum_coef)


def kernel(
    levels, scales, master, momentum,
    out_master, out_momentum, out_w,
    lv, sc, mas, mom, dec, crec, zbuf, zrec, gbuf, grec, ubuf, urec, wbuf, wrec,
    lsem, ssem, msem, css, crs, zss, zrs, gss, grs, uss, urs, wzs, wzr, wcs, wcr, wfs, wfr, wls, wms, osem,
):
    r = lax.axis_index("replica")
    f = lax.axis_index("fsdp")
    x, y, zh = f // 8, (f // 2) % 4, f % 2
    zl, c = r // 2, r % 2
    core = (zl * 2 + (1 - c), f)
    zp = ((1 - zl) * 2 + c, f)
    own = (zl + zh + x // 2) % 2
    same = r == x
    my_slot = (y * 2 + zh) * 2 + c
    my_chunk = x * 4 + y

    def chunk(j):
        return ((x + j // 4) % 4) * 4 + (y + j % 4) % 4

    def sum_owner(j):
        return (x, chunk(j) * 2 + own)

    def row_slot(j):
        return (((y + 4 - j // 4) % 4) * 2 + (zh + j // 2) % 2) * 2 + (c + j) % 2

    def row_owner(j):
        zs = (zh + j // 2) % 2
        return (2 * ((zh + zs + zl) % 2) + (c + j) % 2, r * 8 + ((y + 4 - j // 4) % 4) * 2 + zs)

    bar = pltpu.get_barrier_semaphore()
    pl.semaphore_signal(bar, inc=1, device_id=core, device_id_type=MESH)
    pl.semaphore_signal(bar, inc=1, device_id=zp, device_id_type=MESH)

    def greet(j, _):
        @pl.when(jnp.logical_not(same & (j == 0)))
        def _():
            pl.semaphore_signal(bar, inc=1, device_id=sum_owner(j), device_id_type=MESH)
            pl.semaphore_signal(bar, inc=1, device_id=row_owner(j), device_id_type=MESH)
        return 0

    lax.fori_loop(0, 16, greet, 0)

    def load_scales():
        return pltpu.make_async_copy(scales.at[0], sc, ssem)

    def load_levels(i):
        return pltpu.make_async_copy(levels.at[0, :, pl.ds(i * 1024, 1024)], lv.at[i], lsem.at[i])

    def load_master():
        return pltpu.make_async_copy(master, mas, msem.at[0])

    def load_momentum():
        return pltpu.make_async_copy(momentum, mom, msem.at[1])

    load_scales().start()
    for i in range(LOADS):
        load_levels(i).start()
    load_master().start()
    load_momentum().start()

    load_scales().wait()
    for i in range(LOADS):
        load_levels(i).wait()
        for b in range(4):
            block = i * 4 + b
            for h in range(2):
                at = b * COLS + h * BLOCK
                s = sc[:, 2 * block + h:2 * block + h + 1]
                dec[block, :, h * BLOCK:(h + 1) * BLOCK] = (lv[i, :, at:at + BLOCK].astype(F32) * s).astype(BF16)

    load_master().wait()
    load_momentum().wait()

    def make_u(j, _):
        rows = pl.ds(pl.multiple_of(j * ROWS, ROWS), ROWS)
        ubuf[j] = (mas[rows, :] - MOM * mom[rows, :]).astype(BF16)
        return 0

    lax.fori_loop(0, 16, make_u, 0)

    pl.semaphore_wait(bar, 34 - 2 * same.astype(jnp.int32))

    def remote(src, dst, send, recv, device):
        return pltpu.make_async_remote_copy(
            src_ref=src, dst_ref=dst, send_sem=send, recv_sem=recv, device_id=device, device_id_type=MESH
        )

    mine = pl.ds(pl.multiple_of(c * ROWS, ROWS), ROWS)
    others = pl.ds(pl.multiple_of((1 - c) * ROWS, ROWS), ROWS)

    def core_copy(k):
        return remote(dec.at[pl.ds(2 * k, 2), others, :], crec.at[pl.ds(2 * k, 2)], css.at[k], crs.at[k], core)

    def z_copy(k):
        return remote(zbuf.at[k], zrec.at[k], zss.at[k], zrs.at[k], zp)

    def u_copy(j):
        return remote(ubuf.at[row_slot(j)], urec.at[my_chunk], uss.at[row_slot(j)], urs.at[my_chunk], row_owner(j))

    def u_wait(k):
        return remote(ubuf.at[0], urec.at[k], uss.at[0], urs.at[k], core)

    def g_copy(j):
        return remote(gbuf.at[chunk(j)], grec.at[my_slot], gss.at[chunk(j)], grs.at[my_slot], sum_owner(j))

    def g_wait(s):
        return remote(gbuf.at[0], grec.at[s], gss.at[0], grs.at[s], core)

    def columns(block):
        return pl.ds(pl.multiple_of(block * COLS, COLS), COLS)

    def w_z(k):
        return remote(wbuf.at[k], wrec.at[k], wzs.at[k], wzr.at[k], zp)

    def w_core(k):
        return remote(wbuf.at[k], out_w.at[mine, columns(2 * k + own)], wcs.at[k], wcr.at[k], core)

    def w_local(k):
        return pltpu.make_async_copy(wbuf.at[k], out_w.at[mine, columns(2 * k + own)], wls.at[k])

    def w_forward(k):
        return remote(wrec.at[k], out_w.at[mine, columns(2 * k + 1 - own)], wfs.at[k], wfr.at[k], core)

    def w_keep(k):
        return pltpu.make_async_copy(wrec.at[k], out_w.at[mine, columns(2 * k + 1 - own)], wms.at[k])

    def w_core_wait(k):
        return remote(wbuf.at[k], out_w.at[others, columns(2 * k + own)], wcs.at[k], wcr.at[k], core)

    def w_forward_wait(k):
        return remote(wrec.at[k], out_w.at[others, columns(2 * k + 1 - own)], wfs.at[k], wfr.at[k], core)

    def slot_rows(s):
        return pl.ds(pl.multiple_of(s * ROWS, ROWS), ROWS)

    def put_momentum(s):
        return pltpu.make_async_copy(mom.at[slot_rows(s)], out_momentum.at[slot_rows(s)], osem.at[0, s])

    def put_master(s):
        return pltpu.make_async_copy(mas.at[slot_rows(s)], out_master.at[slot_rows(s)], osem.at[1, s])

    def send_core(j, _):
        core_copy(chunk(j)).start()
        return 0

    lax.fori_loop(0, 16, send_core, 0)

    def send_u(j, _):
        here = same & (j == 0)

        @pl.when(here)
        def _():
            urec[my_chunk] = ubuf[my_slot]

        @pl.when(jnp.logical_not(here))
        def _():
            u_copy(j).start()
        return 0

    def send_z(j, _):
        k = chunk(j)
        b = 2 * k + 1 - own
        core_copy(k).wait_recv()
        zbuf[k] = (dec[b, mine, :].astype(F32) + crec[b].astype(F32)).astype(BF16)
        z_copy(k).start()
        return 0

    lax.fori_loop(0, 4, send_z, 0)
    lax.fori_loop(0, 16, send_u, 0)
    lax.fori_loop(4, 16, send_z, 0)

    def whole(j, _):
        k = chunk(j)
        b = 2 * k + own
        here = same & (j == 0)
        z_copy(k).wait_recv()
        gbuf[k] = (dec[b, mine, :].astype(F32) + crec[b].astype(F32) + zrec[k].astype(F32)).astype(BF16)

        @pl.when(here)
        def _():
            grec[my_slot] = gbuf[k]

        @pl.when(jnp.logical_not(here))
        def _():
            g_copy(j).start()
            u_wait(k).wait_recv()

        total = dec[b, mine, :].astype(F32) + crec[b].astype(F32) + zrec[k].astype(F32)
        wbuf[k] = (urec[k].astype(F32) - (GRAD / 4) * total).astype(BF16)
        w_z(k).start()
        w_core(k).start()
        w_local(k).start()
        return 0

    lax.fori_loop(0, 16, whole, 0)

    def update(j, _):
        s = row_slot(j)
        rows = slot_rows(s)

        @pl.when(jnp.logical_not(same & (j == 0)))
        def _():
            g_wait(s).wait_recv()

        g = grec[s].astype(F32) * 0.25
        new_momentum = momentum_coef * mom[rows, :] + g
        mom[rows, :] = new_momentum
        mas[rows, :] = mas[rows, :] - outer_rate * (g + momentum_coef * new_momentum)
        put_momentum(s).start()
        put_master(s).start()
        return 0

    lax.fori_loop(0, 16, update, 0)

    def pass_on(j, _):
        k = chunk(j)
        w_z(k).wait_recv()
        w_forward(k).start()
        w_keep(k).start()
        return 0

    lax.fori_loop(0, 16, pass_on, 0)

    def finish(j, _):
        k = chunk(j)
        core_copy(k).wait_send()
        z_copy(k).wait_send()

        @pl.when(jnp.logical_not(same & (j == 0)))
        def _():
            u_copy(j).wait_send()
            g_copy(j).wait_send()

        put_momentum(j).wait()
        put_master(j).wait()
        w_z(k).wait_send()
        w_core(k).wait_send()
        w_local(k).wait()
        w_core_wait(k).wait_recv()
        w_forward(k).wait_send()
        w_keep(k).wait()
        w_forward_wait(k).wait_recv()
        return 0

    lax.fori_loop(0, 16, finish, 0)


def per_device(levels, scales, master, momentum):
    small = pltpu.VMEM((CHUNKS, ROWS, COLS), BF16)
    sems = pltpu.SemaphoreType.DMA((16,))
    hbm = pl.BlockSpec(memory_space=pl.ANY)
    return pl.pallas_call(
        kernel,
        out_shape=(
            jax.ShapeDtypeStruct(master.shape, F32),
            jax.ShapeDtypeStruct(momentum.shape, F32),
            jax.ShapeDtypeStruct(levels.shape[1:], BF16),
        ),
        in_specs=[hbm] * 4,
        out_specs=(hbm,) * 3,
        scratch_shapes=[
            pltpu.VMEM((LOADS, 2 * ROWS, 1024), jnp.int32),
            pltpu.VMEM((2 * ROWS, 64), F32),
            pltpu.VMEM(master.shape, F32),
            pltpu.VMEM(momentum.shape, F32),
            pltpu.VMEM((2 * CHUNKS, 2 * ROWS, COLS), BF16),
            pltpu.VMEM((2 * CHUNKS, ROWS, COLS), BF16),
        ]
        + [small] * 8
        + [
            pltpu.SemaphoreType.DMA((LOADS,)),
            pltpu.SemaphoreType.DMA,
            pltpu.SemaphoreType.DMA((2,)),
        ]
        + [sems] * 16
        + [pltpu.SemaphoreType.DMA((2, 16))],
        compiler_params=pltpu.CompilerParams(
            collective_id=0, has_side_effects=True, vmem_limit_bytes=40 * 2**20
        ),
    )(levels, scales, master, momentum)


def solution(mesh):
    in_specs = (
        P("replica", "fsdp", None),
        P("replica", "fsdp", None),
        P("replica", "fsdp"),
        P("replica", "fsdp"),
    )
    out_specs = (P("replica", "fsdp"), P("replica", "fsdp"), P("fsdp", None))
    return jax.shard_map(
        per_device, mesh=mesh, in_specs=in_specs, out_specs=out_specs, check_vma=False
    )
```

```python
import functools

import jax
import jax.numpy as jnp
from jax import lax
from jax.experimental import pallas as pl
from jax.experimental.pallas import tpu as pltpu
from jax.sharding import PartitionSpec as P

MESH = pl.DeviceIdType.MESH
F32 = jnp.float32
BF16 = jnp.bfloat16

BLOCK = 128
ROWS = 128
COLS = 256
CHUNKS = 16
LAG = 3

outer_rate = 0.7
momentum_coef = 0.9
MOM = outer_rate * momentum_coef * momentum_coef
GRAD = outer_rate * (1.0 + momentum_coef)


def kernel(
    levels, scales, master, momentum,
    out_master, out_momentum, out_w,
    lv, sc, sc2, mas, mom, dec, crec, zbuf, zrec, gbuf, grec, ubuf, urec, rel, wbuf, wrec,
    near, far, lsem, ssem, msem, css, crs, zss, zrs, gss, grs, uss, urs, rss, rrs, fss,
    wzs, wzr, wcs, wcr, wfs, wfr, wls, wms, osem,
):
    r = lax.axis_index("replica")
    f = lax.axis_index("fsdp")
    x, y, zh = f // 8, (f // 2) % 4, f % 2
    zl, c = r // 2, r % 2
    core = (zl * 2 + (1 - c), f)
    zp = ((1 - zl) * 2 + c, f)
    cross = (2 * (1 - zl) + c, x * 8 + y * 2 + 1 - zh)
    own = (zl + zh + x // 2) % 2
    same = r == x
    xf = 2 * (1 - zl) + c
    passed = xf == x
    my_slot = (y * 2 + zh) * 2 + c
    my_chunk = x * 4 + y
    leader = r == 0
    herald = r == 3

    def chunk(j):
        b = j % 4
        return ((x + b) % 4) * 4 + (y + j // 4 + b) % 4

    def row_y(i, x_rows):
        return (y + 8 - (x + 4 - x_rows) % 4 - i) % 4

    def row_slot(j):
        return (row_y(j // 4, r) * 2 + (zh + j // 2) % 2) * 2 + (c + j) % 2

    bar = pltpu.get_barrier_semaphore()

    @pl.when(jnp.logical_not(leader))
    def _():
        pl.semaphore_signal(bar, inc=1, device_id=(0, f), device_id_type=MESH)

    def load_scales():
        return pltpu.make_async_copy(scales.at[0], sc, ssem)

    def load_levels(j):
        cols = pl.ds(pl.multiple_of(chunk(j) * 2 * COLS, 2 * COLS), 2 * COLS)
        return pltpu.make_async_copy(levels.at[0, :, cols], lv.at[j], lsem.at[j])

    def load_master():
        return pltpu.make_async_copy(master, mas, msem.at[0])

    def load_momentum():
        return pltpu.make_async_copy(momentum, mom, msem.at[1])

    load_scales().start()

    def load(j, _):
        load_levels(j).start()
        return 0

    lax.fori_loop(0, 16, load, 0)
    load_master().start()
    load_momentum().start()

    @pl.when(leader)
    def _():
        pl.semaphore_wait(bar, 3)
        for member in (1, 2, 3):
            pl.semaphore_signal(near, inc=1, device_id=(member, f), device_id_type=MESH)

    load_scales().wait()
    by_row = jnp.transpose(sc[...])
    sc2[:, :64] = by_row
    sc2[:, 64:] = by_row

    def remote(src, dst, send, recv, device):
        return pltpu.make_async_remote_copy(
            src_ref=src, dst_ref=dst, send_sem=send, recv_sem=recv, device_id=device, device_id_type=MESH
        )

    mine = pl.ds(pl.multiple_of(c * ROWS, ROWS), ROWS)
    others = pl.ds(pl.multiple_of((1 - c) * ROWS, ROWS), ROWS)

    def core_copy(k):
        return remote(dec.at[pl.ds(2 * k, 2), others, :], crec.at[pl.ds(2 * k, 2)], css.at[k], crs.at[k], core)

    def z_copy(k):
        return remote(zbuf.at[k], zrec.at[k], zss.at[k], zrs.at[k], zp)

    def u_copy(i):
        ys, cs = row_y(i // 2, r), (c + i) % 2
        s = (ys * 2 + zh) * 2 + cs
        return remote(ubuf.at[s], urec.at[my_chunk], uss.at[i], urs.at[my_chunk], (2 * zl + cs, r * 8 + ys * 2 + zh))

    def relay_copy(i):
        ys = row_y(i, r)
        return remote(ubuf.at[pl.ds((ys * 2 + 1 - zh) * 2, 2)], rel.at[ys], rss.at[i], rrs.at[ys], cross)

    def relay_wait(i):
        ys = row_y(i, xf)
        return remote(ubuf.at[pl.ds(0, 2)], rel.at[ys], rss.at[i], rrs.at[ys], cross)

    def forward_copy(i):
        ys, cs = row_y(i // 2, xf), (c + i) % 2
        return remote(
            rel.at[ys, cs], urec.at[my_chunk], fss.at[i], urs.at[my_chunk], (2 * zl + cs, xf * 8 + ys * 2 + zh)
        )

    def u_wait(k):
        return remote(ubuf.at[0], urec.at[k], uss.at[0], urs.at[k], core)

    def g_copy(j):
        k = chunk(j)
        return remote(gbuf.at[k], grec.at[my_slot], gss.at[k], grs.at[my_slot], (x, k * 2 + own))

    def g_wait(s):
        return remote(gbuf.at[0], grec.at[s], gss.at[0], grs.at[s], core)

    def columns(block):
        return pl.ds(pl.multiple_of(block * COLS, COLS), COLS)

    def w_z(k):
        return remote(wbuf.at[k], wrec.at[k], wzs.at[k], wzr.at[k], zp)

    def w_core(k):
        return remote(wbuf.at[k], out_w.at[mine, columns(2 * k + own)], wcs.at[k], wcr.at[k], core)

    def w_local(k):
        return pltpu.make_async_copy(wbuf.at[k], out_w.at[mine, columns(2 * k + own)], wls.at[k])

    def w_forward(k):
        return remote(wrec.at[k], out_w.at[mine, columns(2 * k + 1 - own)], wfs.at[k], wfr.at[k], core)

    def w_keep(k):
        return pltpu.make_async_copy(wrec.at[k], out_w.at[mine, columns(2 * k + 1 - own)], wms.at[k])

    def w_core_wait(k):
        return remote(wbuf.at[k], out_w.at[others, columns(2 * k + own)], wcs.at[k], wcr.at[k], core)

    def w_forward_wait(k):
        return remote(wrec.at[k], out_w.at[others, columns(2 * k + 1 - own)], wfs.at[k], wfr.at[k], core)

    def slot_rows(s):
        return pl.ds(pl.multiple_of(s * ROWS, ROWS), ROWS)

    def put_momentum(s):
        return pltpu.make_async_copy(mom.at[slot_rows(s)], out_momentum.at[slot_rows(s)], osem.at[0, s])

    def put_master(s):
        return pltpu.make_async_copy(mas.at[slot_rows(s)], out_master.at[slot_rows(s)], osem.at[1, s])

    def send_z(j):
        k = chunk(j)
        b = 2 * k + 1 - own
        core_copy(k).wait_recv()
        zbuf[k] = (dec[b, mine, :].astype(F32) + crec[b].astype(F32)).astype(BF16)
        z_copy(k).start()

    def first(j, _):
        k = chunk(j)
        load_levels(j).wait()
        s = pltpu.roll(sc2[...], (128 - 4 * k) % 128, 1)
        for h in range(4):
            lanes = slice(h * BLOCK, (h + 1) * BLOCK)
            to = slice(h % 2 * BLOCK, (h % 2 + 1) * BLOCK)
            dec[2 * k + h // 2, :, to] = (lv[j, :, lanes].astype(F32) * s[:, h:h + 1]).astype(BF16)

        @pl.when((j == 0) & jnp.logical_not(leader))
        def _():
            pl.semaphore_wait(near, 1)

        core_copy(k).start()

        @pl.when(herald & (j < 8))
        def _():
            for i in range(4):
                g = (f + 4 * j + i) % 32

                @pl.when(4 * j + i > 0)
                def _():
                    pl.semaphore_signal(bar, inc=1, device_id=(3, g), device_id_type=MESH)

        @pl.when(j >= LAG)
        def _():
            send_z(j - LAG)
        return 0

    lax.fori_loop(0, 16, first, 0)

    def drain(j, _):
        send_z(j)
        return 0

    lax.fori_loop(16 - LAG, 16, drain, 0)

    load_master().wait()
    load_momentum().wait()

    def make_u(j, _):
        rows = pl.ds(pl.multiple_of(j * ROWS, ROWS), ROWS)
        ubuf[j] = (mas[rows, :] - MOM * mom[rows, :]).astype(BF16)
        return 0

    lax.fori_loop(0, 16, make_u, 0)

    @pl.when(herald)
    def _():
        pl.semaphore_wait(bar, 31)
        for member in (0, 1, 2):
            pl.semaphore_signal(far, inc=1, device_id=(member, f), device_id_type=MESH)

    @pl.when(jnp.logical_not(herald))
    def _():
        pl.semaphore_wait(far, 1)

    def send_relay(i, _):
        relay_copy(i).start()
        return 0

    lax.fori_loop(0, 4, send_relay, 0)

    def send_u(i, _):
        here = same & (i == 0)

        @pl.when(here)
        def _():
            urec[my_chunk] = ubuf[my_slot]

        @pl.when(jnp.logical_not(here))
        def _():
            u_copy(i).start()
        return 0

    lax.fori_loop(0, 8, send_u, 0)

    def send_forward(i, _):
        here = passed & (i == 0)

        @pl.when(i % 2 == 0)
        def _():
            relay_wait(i // 2).wait_recv()

        @pl.when(here)
        def _():
            urec[my_chunk] = rel[y, c]

        @pl.when(jnp.logical_not(here))
        def _():
            forward_copy(i).start()
        return 0

    lax.fori_loop(0, 8, send_forward, 0)

    def whole(j, _):
        k = chunk(j)
        b = 2 * k + own
        here = same & (j == 0)
        z_copy(k).wait_recv()
        gbuf[k] = (dec[b, mine, :].astype(F32) + crec[b].astype(F32) + zrec[k].astype(F32)).astype(BF16)

        @pl.when(here)
        def _():
            grec[my_slot] = gbuf[k]

        @pl.when(jnp.logical_not(here))
        def _():
            g_copy(j).start()

        @pl.when(jnp.logical_not((same | passed) & (j == 0)))
        def _():
            u_wait(k).wait_recv()

        total = dec[b, mine, :].astype(F32) + crec[b].astype(F32) + zrec[k].astype(F32)
        wbuf[k] = (urec[k].astype(F32) - (GRAD / 4) * total).astype(BF16)
        w_z(k).start()
        w_core(k).start()
        w_local(k).start()
        return 0

    lax.fori_loop(0, 16, whole, 0)

    def update(j, _):
        s = row_slot(j)
        rows = slot_rows(s)

        @pl.when(jnp.logical_not(same & (j == 0)))
        def _():
            g_wait(s).wait_recv()

        g = grec[s].astype(F32) * 0.25
        new_momentum = momentum_coef * mom[rows, :] + g
        mom[rows, :] = new_momentum
        mas[rows, :] = mas[rows, :] - outer_rate * (g + momentum_coef * new_momentum)
        put_momentum(s).start()
        put_master(s).start()
        return 0

    lax.fori_loop(0, 16, update, 0)

    def over(j):
        k = chunk(j)
        w_z(k).wait_send()
        w_forward(k).wait_send()
        w_keep(k).wait()
        w_forward_wait(k).wait_recv()

    def pass_on(j, _):
        k = chunk(j)
        core_copy(k).wait_send()
        z_copy(k).wait_send()

        @pl.when(jnp.logical_not(same & (j == 0)))
        def _():
            g_copy(j).wait_send()

        @pl.when((j < 8) & jnp.logical_not(same & (j == 0)))
        def _():
            u_copy(j).wait_send()

        @pl.when((j < 8) & jnp.logical_not(passed & (j == 0)))
        def _():
            forward_copy(j).wait_send()

        @pl.when(j < 4)
        def _():
            relay_copy(j).wait_send()

        put_momentum(j).wait()
        put_master(j).wait()
        w_core(k).wait_send()
        w_local(k).wait()
        w_core_wait(k).wait_recv()

        w_z(k).wait_recv()
        w_forward(k).start()
        w_keep(k).start()

        @pl.when(j >= 4)
        def _():
            over(j - 4)
        return 0

    lax.fori_loop(0, 16, pass_on, 0)

    def finish(j, _):
        over(j)
        return 0

    lax.fori_loop(12, 16, finish, 0)


def per_device(levels, scales, master, momentum):
    small = pltpu.VMEM((CHUNKS, ROWS, COLS), BF16)
    sems = pltpu.SemaphoreType.DMA((16,))
    hbm = pl.BlockSpec(memory_space=pltpu.HBM)
    free = pl.BlockSpec(memory_space=pl.ANY)
    return pl.pallas_call(
        kernel,
        out_shape=(
            jax.ShapeDtypeStruct(master.shape, F32),
            jax.ShapeDtypeStruct(momentum.shape, F32),
            jax.ShapeDtypeStruct(levels.shape[1:], BF16),
        ),
        in_specs=[hbm] * 4,
        out_specs=(free,) * 3,
        scratch_shapes=[
            pltpu.VMEM((CHUNKS, 2 * ROWS, 2 * COLS), jnp.int32),
            pltpu.VMEM((64, 2 * ROWS), F32),
            pltpu.VMEM((2 * ROWS, 128), F32),
            pltpu.VMEM(master.shape, F32),
            pltpu.VMEM(momentum.shape, F32),
            pltpu.VMEM((2 * CHUNKS, 2 * ROWS, COLS), BF16),
            pltpu.VMEM((2 * CHUNKS, ROWS, COLS), BF16),
        ]
        + [small] * 6
        + [pltpu.VMEM((4, 2, ROWS, COLS), BF16)]
        + [small] * 2
        + [pltpu.SemaphoreType.REGULAR] * 2
        + [
            sems,
            pltpu.SemaphoreType.DMA,
            pltpu.SemaphoreType.DMA((2,)),
        ]
        + [sems] * 8
        + [pltpu.SemaphoreType.DMA((4,))] * 2
        + [pltpu.SemaphoreType.DMA((8,))]
        + [sems] * 8
        + [pltpu.SemaphoreType.DMA((2, 16))],
        compiler_params=pltpu.CompilerParams(
            collective_id=0, has_side_effects=True, vmem_limit_bytes=40 * 2**20
        ),
    )(*[
        pltpu.with_memory_space_constraint(a, pltpu.HBM)
        for a in (levels, jnp.swapaxes(scales, 1, 2), master, momentum)
    ])


def solution(mesh):
    in_specs = (
        P("replica", "fsdp", None),
        P("replica", "fsdp", None),
        P("replica", "fsdp"),
        P("replica", "fsdp"),
    )
    out_specs = (P("replica", "fsdp"), P("replica", "fsdp"), P("fsdp", None))
    return jax.shard_map(
        per_device, mesh=mesh, in_specs=in_specs, out_specs=out_specs, check_vma=False
    )
```

```python
import functools

import jax
import jax.numpy as jnp
from jax import lax
from jax.experimental import pallas as pl
from jax.experimental.pallas import tpu as pltpu
from jax.sharding import PartitionSpec as P

MESH = pl.DeviceIdType.MESH
F32 = jnp.float32
BF16 = jnp.bfloat16

BLOCK = 128
ROWS = 128
COLS = 256
CHUNKS = 16
AHEAD = 8
LAG = 3

outer_rate = 0.7
momentum_coef = 0.9
MOM = outer_rate * momentum_coef * momentum_coef
GRAD = outer_rate * (1.0 + momentum_coef)


def kernel(
    levels, scales, master, momentum,
    out_master, out_momentum, out_w,
    lv, sc, sc2, mas, mom, dec, crec, zbuf, zrec, gbuf, grec, ubuf, urec, rel, wbuf, wrec,
    near, far, lsem, one, crs, zrs, grs, urs, rrs, wzr,
):
    ssem, masem, mosem, css, zss, gss, uss, rss, fss, wzs, wcs, wcr, wfs, wfr, wls, wms = (one.at[i] for i in range(16))
    r = lax.axis_index("replica")
    f = lax.axis_index("fsdp")
    x, y, zh = f // 8, (f // 2) % 4, f % 2
    zl, c = r // 2, r % 2
    core = (zl * 2 + (1 - c), f)
    zp = ((1 - zl) * 2 + c, f)
    cross = (2 * (1 - zl) + c, x * 8 + y * 2 + 1 - zh)
    own = (zl + zh + x // 2) % 2
    same = r == x
    xf = 2 * (1 - zl) + c
    passed = xf == x
    my_slot = (y * 2 + zh) * 2 + c
    my_chunk = x * 4 + y
    herald = r == 3

    def chunk(j):
        b = j % 4
        return ((x + b) % 4) * 4 + (y + j // 4 + b) % 4

    def row_y(i, x_rows):
        return (y + 8 - (x + 4 - x_rows) % 4 - i) % 4

    bar = pltpu.get_barrier_semaphore()
    for member, greeted in ((0, (1, 2)), (1, (0, 2)), (2, (0,)), (3, (2, 1))):

        @pl.when(r == member)
        def _():
            for other in greeted:
                pl.semaphore_signal(bar, inc=1, device_id=(other, f), device_id_type=MESH)

    def load_scales():
        return pltpu.make_async_copy(scales.at[0], sc, ssem)

    def load_levels(j):
        cols = pl.ds(pl.multiple_of(chunk(j) * 2 * COLS, 2 * COLS), 2 * COLS)
        return pltpu.make_async_copy(levels.at[0, :, cols], lv.at[j], lsem.at[j % AHEAD])

    def load_master():
        return pltpu.make_async_copy(master, mas, masem)

    def load_momentum():
        return pltpu.make_async_copy(momentum, mom, mosem)

    load_scales().start()

    def load(j, _):
        load_levels(j).start()
        return 0

    lax.fori_loop(0, AHEAD, load, 0)
    load_master().start()
    load_momentum().start()

    load_scales().wait()
    by_row = jnp.transpose(sc[...])
    sc2[:, :64] = by_row
    sc2[:, 64:] = by_row

    def remote(src, dst, send, recv, device):
        return pltpu.make_async_remote_copy(
            src_ref=src, dst_ref=dst, send_sem=send, recv_sem=recv, device_id=device, device_id_type=MESH
        )

    def wait_bytes(like, sem):
        pltpu.make_async_copy(like, like, sem).wait()

    mine = pl.ds(pl.multiple_of(c * ROWS, ROWS), ROWS)
    others = pl.ds(pl.multiple_of((1 - c) * ROWS, ROWS), ROWS)

    def core_copy(k):
        return remote(dec.at[pl.ds(2 * k, 2), others, :], crec.at[pl.ds(2 * k, 2)], css, crs.at[k], core)

    def z_copy(k):
        return remote(zbuf.at[k], zrec.at[k], zss, zrs.at[k], zp)

    def u_copy(i):
        ys, cs = row_y(i // 2, r), (c + i) % 2
        s = (ys * 2 + zh) * 2 + cs
        return remote(ubuf.at[s], urec.at[my_chunk], uss, urs.at[i // 2], (2 * zl + cs, r * 8 + ys * 2 + zh))

    def relay_copy(i):
        ys = row_y(i, r)
        return remote(ubuf.at[pl.ds((ys * 2 + 1 - zh) * 2, 2)], rel.at[i], rss, rrs.at[i], cross)

    def forward_copy(i):
        ys, cs = row_y(i // 2, xf), (c + i) % 2
        return remote(
            rel.at[i // 2, cs], urec.at[my_chunk], fss, urs.at[i // 2], (2 * zl + cs, xf * 8 + ys * 2 + zh)
        )

    def g_copy(j):
        k = chunk(j)
        return remote(gbuf.at[k], grec.at[my_slot], gss, grs.at[y], (x, k * 2 + own))

    def columns(block):
        return pl.ds(pl.multiple_of(block * COLS, COLS), COLS)

    def w_z(k):
        return remote(wbuf.at[k], wrec.at[k], wzs, wzr.at[k], zp)

    def w_core(k):
        return remote(wbuf.at[k], out_w.at[mine, columns(2 * k + own)], wcs, wcr, core)

    def w_local(k):
        return pltpu.make_async_copy(wbuf.at[k], out_w.at[mine, columns(2 * k + own)], wls)

    def w_forward(k):
        return remote(wrec.at[k], out_w.at[mine, columns(2 * k + 1 - own)], wfs, wfr, core)

    def w_keep(k):
        return pltpu.make_async_copy(wrec.at[k], out_w.at[mine, columns(2 * k + 1 - own)], wms)

    def slot_rows(s):
        return pl.ds(pl.multiple_of(s * ROWS, ROWS), ROWS)

    def send_z(j):
        k = chunk(j)
        b = 2 * k + 1 - own
        core_copy(k).wait_recv()
        zbuf[k] = (dec[b, mine, :].astype(F32) + crec[b].astype(F32)).astype(BF16)
        z_copy(k).start()

    def make_u(s):
        rows = slot_rows(s)
        ubuf[s] = (mas[rows, :] - MOM * mom[rows, :]).astype(BF16)

    def send_u(i, _):
        here = same & (i == 0)

        @pl.when(here)
        def _():
            urec[my_chunk] = ubuf[my_slot]

        @pl.when(jnp.logical_not(here))
        def _():
            u_copy(i).start()
        return 0

    def first(j, _):
        k = chunk(j)
        load_levels(j).wait()

        @pl.when(j < 16 - AHEAD)
        def _():
            load_levels(j + AHEAD).start()

        s = pltpu.roll(sc2[...], (128 - 4 * k) % 128, 1)
        for h in range(4):
            lanes = slice(h * BLOCK, (h + 1) * BLOCK)
            to = slice(h % 2 * BLOCK, (h % 2 + 1) * BLOCK)
            dec[2 * k + h // 2, :, to] = (lv[j, :, lanes].astype(F32) * s[:, h:h + 1]).astype(BF16)

        @pl.when((j == 0) & (r == 2))
        def _():
            pl.semaphore_wait(bar, 3)
            pl.semaphore_signal(near, inc=1, device_id=(3, f), device_id_type=MESH)

        @pl.when((j == 1) & (r < 2))
        def _():
            pl.semaphore_wait(bar, 2)

        @pl.when((j == 1) & herald)
        def _():
            pl.semaphore_wait(near, 1)

        @pl.when(j == 1)
        def _():
            for i in range(1):
                core_copy(chunk(i)).start()

        @pl.when(j >= 1)
        def _():
            core_copy(k).start()

        @pl.when(herald & (j >= 1) & (j < 1 + 4))
        def _():
            for i in range(8):
                n = 8 * (j - 1) + i

                @pl.when(n > 0)
                def _():
                    pl.semaphore_signal(bar, inc=1, device_id=(3, (f + n) % 32), device_id_type=MESH)

        @pl.when(j >= LAG)
        def _():
            send_z(j - LAG)

        @pl.when(j == 3)
        def _():
            load_master().wait()
            load_momentum().wait()

        @pl.when((j >= 3) & (j < 3 + 4))
        def _():
            for i in range(4):
                make_u(4 * (j - 3) + i)

        @pl.when((j == 8) & herald)
        def _():
            pl.semaphore_wait(bar, 31)
            for member in (0, 1, 2):
                pl.semaphore_signal(far, inc=1, device_id=(member, f), device_id_type=MESH)

        @pl.when((j == 8) & jnp.logical_not(herald))
        def _():
            pl.semaphore_wait(far, 1)

        @pl.when(j == 8)
        def _():
            for i in range(4):
                relay_copy(i).start()
            lax.fori_loop(0, 8, send_u, 0)
        return 0

    lax.fori_loop(0, 16, first, 0)

    def drain(j, _):
        send_z(j)
        return 0

    lax.fori_loop(16 - LAG, 16, drain, 0)

    def send_forward(i, _):
        here = passed & (i == 0)

        @pl.when(i % 2 == 0)
        def _():
            relay_copy(i // 2).wait_recv()

        @pl.when(here)
        def _():
            urec[my_chunk] = rel[0, c]

        @pl.when(jnp.logical_not(here))
        def _():
            forward_copy(i).start()
        return 0

    lax.fori_loop(0, 8, send_forward, 0)

    def whole(j, _):
        k = chunk(j)
        b = 2 * k + own
        here = same & (j == 0)
        z_copy(k).wait_recv()
        gbuf[k] = (dec[b, mine, :].astype(F32) + crec[b].astype(F32) + zrec[k].astype(F32)).astype(BF16)

        @pl.when(here)
        def _():
            grec[my_slot] = gbuf[k]

        @pl.when(jnp.logical_not(here))
        def _():
            g_copy(j).start()

        local = (same | passed) & (j == 0)

        @pl.when(local)
        def _():
            wait_bytes(urec.at[pl.ds(0, 3)], urs.at[0])

        @pl.when((j % 4 == 0) & jnp.logical_not(local))
        def _():
            wait_bytes(urec.at[pl.ds(0, 4)], urs.at[j // 4])

        total = dec[b, mine, :].astype(F32) + crec[b].astype(F32) + zrec[k].astype(F32)
        wbuf[k] = (urec[k].astype(F32) - (GRAD / 4) * total).astype(BF16)
        w_z(k).start()
        w_core(k).start()
        w_local(k).start()
        return 0

    lax.fori_loop(0, 16, whole, 0)

    def update(i, _):
        ys = row_y(i, r)
        local = same & (i == 0)

        @pl.when(local)
        def _():
            wait_bytes(grec.at[pl.ds(0, 3)], grs.at[ys])

        @pl.when(jnp.logical_not(local))
        def _():
            wait_bytes(grec.at[pl.ds(0, 4)], grs.at[ys])

        for n in range(4):
            s = ys * 4 + n
            rows = slot_rows(s)
            g = grec[s].astype(F32) * 0.25
            new_momentum = momentum_coef * mom[rows, :] + g
            mom[rows, :] = new_momentum
            mas[rows, :] = mas[rows, :] - outer_rate * (g + momentum_coef * new_momentum)
        rows = pl.ds(pl.multiple_of(ys * 4 * ROWS, ROWS), 4 * ROWS)
        pltpu.make_async_copy(mom.at[rows], out_momentum.at[rows], mosem).start()
        pltpu.make_async_copy(mas.at[rows], out_master.at[rows], masem).start()
        return 0

    lax.fori_loop(0, 4, update, 0)

    def pass_on(j, _):
        k = chunk(j)
        w_z(k).wait_recv()
        w_forward(k).start()
        w_keep(k).start()
        return 0

    lax.fori_loop(0, 16, pass_on, 0)

    wait_bytes(crec, css)
    wait_bytes(zbuf, zss)
    wait_bytes(rel, rss)
    for sem, buf, blocks, less in ((uss, ubuf, 8, same), (fss, ubuf, 8, passed), (gss, gbuf, 16, same)):

        @pl.when(less)
        def _():
            wait_bytes(buf.at[pl.ds(0, blocks - 1)], sem)

        @pl.when(jnp.logical_not(less))
        def _():
            wait_bytes(buf.at[pl.ds(0, blocks)], sem)

    wait_bytes(mom, mosem)
    wait_bytes(mas, masem)
    for sem in (wcs, wls, wcr, wzs, wms, wfs, wfr):
        wait_bytes(wbuf, sem)


def write_kernel(a, b, w, out_a, out_b, out_w, sems):
    copies = [
        pltpu.make_async_copy(a, out_a, sems.at[0]),
        pltpu.make_async_copy(b, out_b, sems.at[1]),
    ]
    copies += [
        pltpu.make_async_copy(w.at[pl.ds(i * 64, 64)], out_w.at[pl.ds(i * 64, 64)], sems.at[2 + i]) for i in range(4)
    ]
    for copy in copies:
        copy.start()
    for copy in copies:
        copy.wait()


def write(*results):
    free = pl.BlockSpec(memory_space=pl.ANY)
    return pl.pallas_call(
        write_kernel,
        out_shape=tuple(jax.ShapeDtypeStruct(a.shape, a.dtype) for a in results),
        in_specs=[free] * 3,
        out_specs=(free,) * 3,
        scratch_shapes=[pltpu.SemaphoreType.DMA((6,))],
        compiler_params=pltpu.CompilerParams(vmem_limit_bytes=1 * 2**20),
    )(*results)


def per_device(levels, scales, master, momentum):
    small = pltpu.VMEM((CHUNKS, ROWS, COLS), BF16)
    free = pl.BlockSpec(memory_space=pl.ANY)
    return write(*pl.pallas_call(
        kernel,
        out_shape=(
            jax.ShapeDtypeStruct(master.shape, F32),
            jax.ShapeDtypeStruct(momentum.shape, F32),
            jax.ShapeDtypeStruct(levels.shape[1:], BF16),
        ),
        in_specs=[pl.BlockSpec(memory_space=pltpu.HBM)] * 4,
        out_specs=(free,) * 3,
        scratch_shapes=[
            pltpu.VMEM((CHUNKS, 2 * ROWS, 2 * COLS), jnp.int32),
            pltpu.VMEM((64, 2 * ROWS), F32),
            pltpu.VMEM((2 * ROWS, 128), F32),
            pltpu.VMEM(master.shape, F32),
            pltpu.VMEM(momentum.shape, F32),
            pltpu.VMEM((2 * CHUNKS, 2 * ROWS, COLS), BF16),
            pltpu.VMEM((2 * CHUNKS, ROWS, COLS), BF16),
        ]
        + [small] * 6
        + [pltpu.VMEM((4, 2, ROWS, COLS), BF16)]
        + [small] * 2
        + [pltpu.SemaphoreType.REGULAR] * 2
        + [pltpu.SemaphoreType.DMA((n,)) for n in (AHEAD, 16, 16, 16, 4, 4, 4, 16)],
        compiler_params=pltpu.CompilerParams(
            collective_id=0, has_side_effects=True, vmem_limit_bytes=40 * 2**20
        ),
    )(*[
        pltpu.with_memory_space_constraint(a, pltpu.HBM)
        for a in (levels, jnp.swapaxes(scales, 1, 2), master, momentum)
    ]))


def solution(mesh):
    in_specs = (
        P("replica", "fsdp", None),
        P("replica", "fsdp", None),
        P("replica", "fsdp"),
        P("replica", "fsdp"),
    )
    out_specs = (P("replica", "fsdp"), P("replica", "fsdp"), P("fsdp", None))
    return jax.shard_map(
        per_device, mesh=mesh, in_specs=in_specs, out_specs=out_specs, check_vma=False
    )
```

```python
import functools

import jax
import jax.numpy as jnp
from jax import lax
from jax.experimental import pallas as pl
from jax.experimental.pallas import tpu as pltpu
from jax.sharding import PartitionSpec as P

MESH = pl.DeviceIdType.MESH
F32 = jnp.float32
BF16 = jnp.bfloat16

BLOCK = 128
ROWS = 128
COLS = 256
CHUNKS = 16
AHEAD = 8
LAG = 2

outer_rate = 0.7
momentum_coef = 0.9
MOM = outer_rate * momentum_coef * momentum_coef
GRAD = outer_rate * (1.0 + momentum_coef)


def kernel(
    levels, scales, master, momentum,
    out_master, out_momentum, out_w,
    lv, sc, sc2, mas, mom, dec, crec, zbuf, zrec, gbuf, grec, ubuf, urec, rel, wbuf, wrec,
    near, far, lsem, one, crs, zrs, grs, urs, rrs, wzr,
):
    ssem, masem, mosem, css, zss, gss, uss, rss, fss, wzs, wcs, wcr, wfs, wfr, wls, wms = (one.at[i] for i in range(16))
    r = lax.axis_index("replica")
    f = lax.axis_index("fsdp")
    x, y, zh = f // 8, (f // 2) % 4, f % 2
    zl, c = r // 2, r % 2
    core = (zl * 2 + (1 - c), f)
    zp = ((1 - zl) * 2 + c, f)
    cross = (2 * (1 - zl) + c, x * 8 + y * 2 + 1 - zh)
    own = (zl + zh + x // 2) % 2
    same = r == x
    xf = 2 * (1 - zl) + c
    passed = xf == x
    my_slot = (y * 2 + zh) * 2 + c
    my_chunk = x * 4 + y
    herald = r == 0

    def chunk(j):
        b = j % 4
        return ((x + b) % 4) * 4 + (y + j // 4 + b) % 4

    def row_y(i, x_rows):
        return (y + 8 - (x + 4 - x_rows) % 4 - i) % 4

    bar = pltpu.get_barrier_semaphore()
    def load_scales():
        return pltpu.make_async_copy(scales.at[0], sc, ssem)

    def load_levels(j):
        cols = pl.ds(pl.multiple_of(chunk(j) * 2 * COLS, 2 * COLS), 2 * COLS)
        return pltpu.make_async_copy(levels.at[0, :, cols], lv.at[j], lsem.at[j % AHEAD])

    def load_master():
        return pltpu.make_async_copy(master, mas, masem)

    def load_momentum():
        return pltpu.make_async_copy(momentum, mom, mosem)

    load_scales().start()

    def load(j, _):
        load_levels(j).start()
        return 0

    load_levels(0).start()

    for member, greeted in ((0, (1, 2, 3)), (1, (2, 3)), (2, (1, 3)), (3, (1, 2))):

        @pl.when(r == member)
        def _():
            for other in greeted:
                pl.semaphore_signal(bar, inc=1, device_id=(other, f), device_id_type=MESH)

    lax.fori_loop(1, AHEAD, load, 0)
    load_master().start()
    load_momentum().start()

    load_scales().wait()
    by_row = jnp.transpose(sc[...])
    sc2[:, :64] = by_row
    sc2[:, 64:] = by_row

    def remote(src, dst, send, recv, device):
        return pltpu.make_async_remote_copy(
            src_ref=src, dst_ref=dst, send_sem=send, recv_sem=recv, device_id=device, device_id_type=MESH
        )

    def wait_bytes(like, sem):
        pltpu.make_async_copy(like, like, sem).wait()

    mine = pl.ds(pl.multiple_of(c * ROWS, ROWS), ROWS)
    others = pl.ds(pl.multiple_of((1 - c) * ROWS, ROWS), ROWS)

    def core_copy(k):
        return remote(dec.at[pl.ds(2 * k, 2), others, :], crec.at[pl.ds(2 * k, 2)], css, crs.at[k], core)

    def z_copy(k):
        return remote(zbuf.at[k], zrec.at[k], zss, zrs.at[k], zp)

    def u_copy(i):
        ys, cs = row_y(i // 2, r), (c + i) % 2
        s = (ys * 2 + zh) * 2 + cs
        return remote(ubuf.at[s], urec.at[my_chunk], uss, urs.at[i // 2], (2 * zl + cs, r * 8 + ys * 2 + zh))

    def relay_copy(i):
        ys = row_y(i, r)
        return remote(ubuf.at[pl.ds((ys * 2 + 1 - zh) * 2, 2)], rel.at[i], rss, rrs.at[i], cross)

    def forward_copy(i):
        ys, cs = row_y(i // 2, xf), (c + i) % 2
        return remote(
            rel.at[i // 2, cs], urec.at[my_chunk], fss, urs.at[i // 2], (2 * zl + cs, xf * 8 + ys * 2 + zh)
        )

    def g_copy(j):
        k = chunk(j)
        return remote(gbuf.at[k], grec.at[my_slot], gss, grs.at[y], (x, k * 2 + own))

    def columns(block):
        return pl.ds(pl.multiple_of(block * COLS, COLS), COLS)

    def w_z(k):
        return remote(wbuf.at[k], wrec.at[k], wzs, wzr.at[k], zp)

    def w_core(k):
        return remote(wbuf.at[k], out_w.at[mine, columns(2 * k + own)], wcs, wcr, core)

    def w_local(k):
        return pltpu.make_async_copy(wbuf.at[k], out_w.at[mine, columns(2 * k + own)], wls)

    def w_forward(k):
        return remote(wrec.at[k], out_w.at[mine, columns(2 * k + 1 - own)], wfs, wfr, core)

    def w_keep(k):
        return pltpu.make_async_copy(wrec.at[k], out_w.at[mine, columns(2 * k + 1 - own)], wms)

    def slot_rows(s):
        return pl.ds(pl.multiple_of(s * ROWS, ROWS), ROWS)

    def send_z(j):
        k = chunk(j)
        b = 2 * k + 1 - own
        core_copy(k).wait_recv()
        zbuf[k] = (dec[b, mine, :].astype(F32) + crec[b].astype(F32)).astype(BF16)
        z_copy(k).start()

    def make_u(s):
        rows = slot_rows(s)
        ubuf[s] = (mas[rows, :] - MOM * mom[rows, :]).astype(BF16)

    def send_u(i, _):
        here = same & (i == 0)

        @pl.when(here)
        def _():
            urec[my_chunk] = ubuf[my_slot]

        @pl.when(jnp.logical_not(here))
        def _():
            u_copy(i).start()
        return 0

    def first(j, _):
        k = chunk(j)
        load_levels(j).wait()

        @pl.when(j < 16 - AHEAD)
        def _():
            load_levels(j + AHEAD).start()

        s = pltpu.roll(sc2[...], (128 - 4 * k) % 128, 1)
        for h in range(4):
            lanes = slice(h * BLOCK, (h + 1) * BLOCK)
            to = slice(h % 2 * BLOCK, (h % 2 + 1) * BLOCK)
            dec[2 * k + h // 2, :, to] = (lv[j, :, lanes].astype(F32) * s[:, h:h + 1]).astype(BF16)

        @pl.when((j == 0) & jnp.logical_not(herald))
        def _():
            pl.semaphore_wait(bar, 3)

        @pl.when((j == 0) & (r == 1))
        def _():
            pl.semaphore_signal(near, inc=1, device_id=(0, f), device_id_type=MESH)

        @pl.when((j == 0) & herald)
        def _():
            pl.semaphore_wait(near, 1)

        core_copy(k).start()

        @pl.when(j >= LAG)
        def _():
            send_z(j - LAG)

        @pl.when((j >= 1) & (j < 5))
        def _():
            for i in range(2):
                n = 8 * r + 2 * (j - 1) + i

                @pl.when(n > 0)
                def _():
                    pl.semaphore_signal(bar, inc=1, device_id=(0, (f + n) % 32), device_id_type=MESH)

        @pl.when(j == 3)
        def _():
            load_master().wait()
            load_momentum().wait()

        @pl.when((j >= 3) & (j < 3 + 4))
        def _():
            for i in range(4):
                make_u(4 * (j - 3) + i)

        @pl.when((j == 8) & herald)
        def _():
            pl.semaphore_wait(bar, 31)
            for member in (1, 2, 3):
                pl.semaphore_signal(far, inc=1, device_id=(member, f), device_id_type=MESH)

        @pl.when((j == 8) & jnp.logical_not(herald))
        def _():
            pl.semaphore_wait(far, 1)

        @pl.when(j == 8)
        def _():
            for i in range(4):
                relay_copy(i).start()
            lax.fori_loop(0, 8, send_u, 0)
        return 0

    lax.fori_loop(0, 16, first, 0)

    def drain(j, _):
        send_z(j)
        return 0

    lax.fori_loop(16 - LAG, 16, drain, 0)

    def send_forward(i, _):
        here = passed & (i == 0)

        @pl.when(i % 2 == 0)
        def _():
            relay_copy(i // 2).wait_recv()

        @pl.when(here)
        def _():
            urec[my_chunk] = rel[0, c]

        @pl.when(jnp.logical_not(here))
        def _():
            forward_copy(i).start()
        return 0

    lax.fori_loop(0, 8, send_forward, 0)

    def whole(j, _):
        k = chunk(j)
        b = 2 * k + own
        here = same & (j == 0)
        z_copy(k).wait_recv()
        gbuf[k] = (dec[b, mine, :].astype(F32) + crec[b].astype(F32) + zrec[k].astype(F32)).astype(BF16)

        @pl.when(here)
        def _():
            grec[my_slot] = gbuf[k]

        @pl.when(jnp.logical_not(here))
        def _():
            g_copy(j).start()

        local = (same | passed) & (j == 0)

        @pl.when(local)
        def _():
            wait_bytes(urec.at[pl.ds(0, 3)], urs.at[0])

        @pl.when((j % 4 == 0) & jnp.logical_not(local))
        def _():
            wait_bytes(urec.at[pl.ds(0, 4)], urs.at[j // 4])

        total = dec[b, mine, :].astype(F32) + crec[b].astype(F32) + zrec[k].astype(F32)
        wbuf[k] = (urec[k].astype(F32) - (GRAD / 4) * total).astype(BF16)
        w_z(k).start()
        w_core(k).start()
        w_local(k).start()
        return 0

    lax.fori_loop(0, 16, whole, 0)

    def update(i, _):
        ys = row_y(i, r)
        local = same & (i == 0)

        @pl.when(local)
        def _():
            wait_bytes(grec.at[pl.ds(0, 3)], grs.at[ys])

        @pl.when(jnp.logical_not(local))
        def _():
            wait_bytes(grec.at[pl.ds(0, 4)], grs.at[ys])

        for n in range(4):
            s = ys * 4 + n
            rows = slot_rows(s)
            g = grec[s].astype(F32) * 0.25
            new_momentum = momentum_coef * mom[rows, :] + g
            mom[rows, :] = new_momentum
            mas[rows, :] = mas[rows, :] - outer_rate * (g + momentum_coef * new_momentum)
        rows = pl.ds(pl.multiple_of(ys * 4 * ROWS, ROWS), 4 * ROWS)
        pltpu.make_async_copy(mom.at[rows], out_momentum.at[rows], mosem).start()
        pltpu.make_async_copy(mas.at[rows], out_master.at[rows], masem).start()
        return 0

    lax.fori_loop(0, 4, update, 0)

    def pass_on(j, _):
        k = chunk(j)
        w_z(k).wait_recv()
        w_forward(k).start()
        w_keep(k).start()
        return 0

    lax.fori_loop(0, 16, pass_on, 0)

    wait_bytes(crec, css)
    wait_bytes(zbuf, zss)
    wait_bytes(rel, rss)
    for sem, buf, blocks, less in ((uss, ubuf, 8, same), (fss, ubuf, 8, passed), (gss, gbuf, 16, same)):

        @pl.when(less)
        def _():
            wait_bytes(buf.at[pl.ds(0, blocks - 1)], sem)

        @pl.when(jnp.logical_not(less))
        def _():
            wait_bytes(buf.at[pl.ds(0, blocks)], sem)

    wait_bytes(mom, mosem)
    wait_bytes(mas, masem)
    for sem in (wcs, wls, wcr, wzs, wms, wfs, wfr):
        wait_bytes(wbuf, sem)


def write_kernel(a, b, w, out_a, out_b, out_w, sems):
    copies = [
        pltpu.make_async_copy(a, out_a, sems.at[0]),
        pltpu.make_async_copy(b, out_b, sems.at[1]),
    ]
    copies += [
        pltpu.make_async_copy(w.at[pl.ds(i * 64, 64)], out_w.at[pl.ds(i * 64, 64)], sems.at[2 + i]) for i in range(4)
    ]
    for copy in copies:
        copy.start()
    for copy in copies:
        copy.wait()


def write(*results):
    free = pl.BlockSpec(memory_space=pl.ANY)
    return pl.pallas_call(
        write_kernel,
        out_shape=tuple(jax.ShapeDtypeStruct(a.shape, a.dtype) for a in results),
        in_specs=[free] * 3,
        out_specs=(free,) * 3,
        scratch_shapes=[pltpu.SemaphoreType.DMA((6,))],
        compiler_params=pltpu.CompilerParams(vmem_limit_bytes=1 * 2**20),
    )(*results)


def per_device(levels, scales, master, momentum):
    small = pltpu.VMEM((CHUNKS, ROWS, COLS), BF16)
    free = pl.BlockSpec(memory_space=pl.ANY)
    return write(*pl.pallas_call(
        kernel,
        out_shape=(
            jax.ShapeDtypeStruct(master.shape, F32),
            jax.ShapeDtypeStruct(momentum.shape, F32),
            jax.ShapeDtypeStruct(levels.shape[1:], BF16),
        ),
        in_specs=[pl.BlockSpec(memory_space=pltpu.HBM)] * 4,
        out_specs=(free,) * 3,
        scratch_shapes=[
            pltpu.VMEM((CHUNKS, 2 * ROWS, 2 * COLS), jnp.int32),
            pltpu.VMEM((64, 2 * ROWS), F32),
            pltpu.VMEM((2 * ROWS, 128), F32),
            pltpu.VMEM(master.shape, F32),
            pltpu.VMEM(momentum.shape, F32),
            pltpu.VMEM((2 * CHUNKS, 2 * ROWS, COLS), BF16),
            pltpu.VMEM((2 * CHUNKS, ROWS, COLS), BF16),
        ]
        + [small] * 6
        + [pltpu.VMEM((4, 2, ROWS, COLS), BF16)]
        + [small] * 2
        + [pltpu.SemaphoreType.REGULAR] * 2
        + [pltpu.SemaphoreType.DMA((n,)) for n in (AHEAD, 16, 16, 16, 4, 4, 4, 16)],
        compiler_params=pltpu.CompilerParams(
            collective_id=0, has_side_effects=True, vmem_limit_bytes=40 * 2**20
        ),
    )(*[
        pltpu.with_memory_space_constraint(a, pltpu.HBM)
        for a in (levels, jnp.swapaxes(scales, 1, 2), master, momentum)
    ]))


def solution(mesh):
    in_specs = (
        P("replica", "fsdp", None),
        P("replica", "fsdp", None),
        P("replica", "fsdp"),
        P("replica", "fsdp"),
    )
    out_specs = (P("replica", "fsdp"), P("replica", "fsdp"), P("fsdp", None))
    return jax.shard_map(
        per_device, mesh=mesh, in_specs=in_specs, out_specs=out_specs, check_vma=False
    )
```

```python
import functools

import jax
import jax.numpy as jnp
from jax import lax
from jax.experimental import pallas as pl
from jax.experimental.pallas import tpu as pltpu
from jax.sharding import PartitionSpec as P

MESH = pl.DeviceIdType.MESH
F32 = jnp.float32
BF16 = jnp.bfloat16

BLOCK = 128
ROWS = 128
COLS = 256
CHUNKS = 16
HEAD = 128
AHEAD = 8
LAG = 2

outer_rate = 0.7
momentum_coef = 0.9
MOM = outer_rate * momentum_coef * momentum_coef
GRAD = outer_rate * (1.0 + momentum_coef)


def kernel(
    levels, scales, master, momentum,
    out_master, out_momentum, out_w,
    lv, sc, sc2, mas, mom, dec, crec, zbuf, zrec, gbuf, grec, ubuf, urec, rel, wbuf, wrec, zraw,
    near, far, lsem, one, crs, zrs, grs, urs, rrs, wzr,
):
    ssem, masem, mosem, css, zss, gss, uss, rss, fss, wzs, wcs, wcr, wfs, wfr, wls, wms, xss, xrs = (
        one.at[i] for i in range(18)
    )
    r = lax.axis_index("replica")
    f = lax.axis_index("fsdp")
    x, y, zh = f // 8, (f // 2) % 4, f % 2
    zl, c = r // 2, r % 2
    core = (zl * 2 + (1 - c), f)
    zp = ((1 - zl) * 2 + c, f)
    zd = ((1 - zl) * 2 + (1 - c), f)
    cross = (2 * (1 - zl) + c, x * 8 + y * 2 + 1 - zh)
    own = (zl + zh + x // 2) % 2
    same = r == x
    xf = 2 * (1 - zl) + c
    passed = xf == x
    my_slot = (y * 2 + zh) * 2 + c
    my_chunk = x * 4 + y
    herald = r == 0

    def chunk(j):
        b = j % 4
        return ((x + b) % 4) * 4 + (y + j // 4 + b) % 4

    def row_y(i, x_rows):
        return (y + 8 - (x + 4 - x_rows) % 4 - i) % 4

    bar = pltpu.get_barrier_semaphore()
    def load_scales():
        return pltpu.make_async_copy(scales.at[0], sc, ssem)

    def load_levels(j):
        cols = pl.ds(pl.multiple_of(chunk(j) * 2 * COLS, 2 * COLS), 2 * COLS)
        return pltpu.make_async_copy(levels.at[0, :, cols], lv.at[j], lsem.at[j % AHEAD])

    def load_master():
        return pltpu.make_async_copy(master, mas, masem)

    def load_momentum():
        return pltpu.make_async_copy(momentum, mom, mosem)

    load_scales().start()

    def load(j, _):
        load_levels(j).start()
        return 0

    load_levels(0).start()

    for member, greeted in ((0, (1, 2, 3)), (1, (2, 3)), (2, (1, 3)), (3, (1, 2))):

        @pl.when(r == member)
        def _():
            for other in greeted:
                pl.semaphore_signal(bar, inc=1, device_id=(other, f), device_id_type=MESH)

    lax.fori_loop(1, AHEAD, load, 0)
    load_master().start()
    load_momentum().start()

    load_scales().wait()
    by_row = jnp.transpose(sc[...])
    sc2[:, :64] = by_row
    sc2[:, 64:] = by_row

    def remote(src, dst, send, recv, device):
        return pltpu.make_async_remote_copy(
            src_ref=src, dst_ref=dst, send_sem=send, recv_sem=recv, device_id=device, device_id_type=MESH
        )

    def wait_bytes(like, sem):
        pltpu.make_async_copy(like, like, sem).wait()

    mine = pl.ds(pl.multiple_of(c * ROWS, ROWS), ROWS)
    others = pl.ds(pl.multiple_of((1 - c) * ROWS, ROWS), ROWS)

    def core_copy(k):
        return remote(dec.at[pl.ds(2 * k, 2), others, :], crec.at[pl.ds(2 * k, 2)], css, crs.at[k], core)

    def z_copy(k):
        return remote(zbuf.at[k], zrec.at[k], zss, zrs.at[k], zp)

    def head_copy(k):
        b = 2 * k + 1 - own
        return remote(dec.at[b, mine, pl.ds(0, HEAD)], zrec.at[k, :, pl.ds(0, HEAD)], zss, zrs.at[k], zp)

    def other_head_copy(k):
        return remote(dec.at[2 * k + 1 - own, others, pl.ds(0, HEAD)], zraw, xss, xrs, zd)

    def rest_copy(k):
        cols = pl.ds(HEAD, COLS - HEAD)
        return remote(zbuf.at[k, :, cols], zrec.at[k, :, cols], zss, zrs.at[k], zp)

    def u_copy(i):
        ys, cs = row_y(i // 2, r), (c + i) % 2
        s = (ys * 2 + zh) * 2 + cs
        return remote(ubuf.at[s], urec.at[my_chunk], uss, urs.at[i // 2], (2 * zl + cs, r * 8 + ys * 2 + zh))

    def relay_copy(i):
        ys = row_y(i, r)
        return remote(ubuf.at[pl.ds((ys * 2 + 1 - zh) * 2, 2)], rel.at[i], rss, rrs.at[i], cross)

    def forward_copy(i):
        ys, cs = row_y(i // 2, xf), (c + i) % 2
        return remote(
            rel.at[i // 2, cs], urec.at[my_chunk], fss, urs.at[i // 2], (2 * zl + cs, xf * 8 + ys * 2 + zh)
        )

    def g_copy(j):
        k = chunk(j)
        return remote(gbuf.at[k], grec.at[my_slot], gss, grs.at[y], (x, k * 2 + own))

    def columns(block):
        return pl.ds(pl.multiple_of(block * COLS, COLS), COLS)

    def w_z(k):
        return remote(wbuf.at[k], wrec.at[k], wzs, wzr.at[k], zp)

    def w_core(k):
        return remote(wbuf.at[k], out_w.at[mine, columns(2 * k + own)], wcs, wcr, core)

    def w_local(k):
        return pltpu.make_async_copy(wbuf.at[k], out_w.at[mine, columns(2 * k + own)], wls)

    def w_forward(k):
        return remote(wrec.at[k], out_w.at[mine, columns(2 * k + 1 - own)], wfs, wfr, core)

    def w_keep(k):
        return pltpu.make_async_copy(wrec.at[k], out_w.at[mine, columns(2 * k + 1 - own)], wms)

    def slot_rows(s):
        return pl.ds(pl.multiple_of(s * ROWS, ROWS), ROWS)

    def send_z(j):
        k = chunk(j)
        b = 2 * k + 1 - own
        core_copy(k).wait_recv()
        zbuf[k] = (dec[b, mine, :].astype(F32) + crec[b].astype(F32)).astype(BF16)

        @pl.when(j == 0)
        def _():
            rest_copy(k).start()

        @pl.when(j > 0)
        def _():
            z_copy(k).start()

    def make_u(s):
        rows = slot_rows(s)
        ubuf[s] = (mas[rows, :] - MOM * mom[rows, :]).astype(BF16)

    def send_u(i, _):
        here = same & (i == 0)

        @pl.when(here)
        def _():
            urec[my_chunk] = ubuf[my_slot]

        @pl.when(jnp.logical_not(here))
        def _():
            u_copy(i).start()
        return 0

    def first(j, _):
        k = chunk(j)
        load_levels(j).wait()

        @pl.when(j < 16 - AHEAD)
        def _():
            load_levels(j + AHEAD).start()

        s = pltpu.roll(sc2[...], (128 - 4 * k) % 128, 1)
        for h in range(4):
            lanes = slice(h * BLOCK, (h + 1) * BLOCK)
            to = slice(h % 2 * BLOCK, (h % 2 + 1) * BLOCK)
            dec[2 * k + h // 2, :, to] = (lv[j, :, lanes].astype(F32) * s[:, h:h + 1]).astype(BF16)

        @pl.when((j == 0) & jnp.logical_not(herald))
        def _():
            pl.semaphore_wait(bar, 3)

        @pl.when((j == 0) & (r == 1))
        def _():
            pl.semaphore_signal(near, inc=1, device_id=(0, f), device_id_type=MESH)

        @pl.when((j == 0) & herald)
        def _():
            pl.semaphore_wait(near, 1)

        @pl.when(j == 0)
        def _():
            head_copy(k).start()
            other_head_copy(k).start()

        core_copy(k).start()

        @pl.when(j >= LAG)
        def _():
            send_z(j - LAG)

        @pl.when((j >= 1) & (j < 5))
        def _():
            for i in range(2):
                n = 8 * r + 2 * (j - 1) + i

                @pl.when(n > 0)
                def _():
                    pl.semaphore_signal(bar, inc=1, device_id=(0, (f + n) % 32), device_id_type=MESH)

        @pl.when(j == 3)
        def _():
            load_master().wait()
            load_momentum().wait()

        @pl.when((j >= 3) & (j < 3 + 4))
        def _():
            for i in range(4):
                make_u(4 * (j - 3) + i)

        @pl.when((j == 12) & herald)
        def _():
            pl.semaphore_wait(bar, 31)
            for member in (1, 2, 3):
                pl.semaphore_signal(far, inc=1, device_id=(member, f), device_id_type=MESH)

        @pl.when((j == 12) & jnp.logical_not(herald))
        def _():
            pl.semaphore_wait(far, 1)

        @pl.when(j == 12)
        def _():
            for i in range(4):
                relay_copy(i).start()
            lax.fori_loop(0, 8, send_u, 0)
        return 0

    lax.fori_loop(0, 16, first, 0)

    def drain(j, _):
        send_z(j)
        return 0

    lax.fori_loop(16 - LAG, 16, drain, 0)

    def send_forward(i, _):
        here = passed & (i == 0)

        @pl.when(i % 2 == 0)
        def _():
            relay_copy(i // 2).wait_recv()

        @pl.when(here)
        def _():
            urec[my_chunk] = rel[0, c]

        @pl.when(jnp.logical_not(here))
        def _():
            forward_copy(i).start()
        return 0

    lax.fori_loop(0, 8, send_forward, 0)

    def whole(j, _):
        k = chunk(j)
        b = 2 * k + own
        here = same & (j == 0)
        z_copy(k).wait_recv()

        @pl.when(j == 0)
        def _():
            other_head_copy(k).wait_recv()
            zrec[k, :, :HEAD] = (zrec[k, :, :HEAD].astype(F32) + zraw[...].astype(F32)).astype(BF16)

        gbuf[k] = (dec[b, mine, :].astype(F32) + crec[b].astype(F32) + zrec[k].astype(F32)).astype(BF16)

        @pl.when(here)
        def _():
            grec[my_slot] = gbuf[k]

        @pl.when(jnp.logical_not(here))
        def _():
            g_copy(j).start()

        local = (same | passed) & (j == 0)

        @pl.when(local)
        def _():
            wait_bytes(urec.at[pl.ds(0, 3)], urs.at[0])

        @pl.when((j % 4 == 0) & jnp.logical_not(local))
        def _():
            wait_bytes(urec.at[pl.ds(0, 4)], urs.at[j // 4])

        total = dec[b, mine, :].astype(F32) + crec[b].astype(F32) + zrec[k].astype(F32)
        wbuf[k] = (urec[k].astype(F32) - (GRAD / 4) * total).astype(BF16)
        w_z(k).start()
        w_core(k).start()
        w_local(k).start()
        return 0

    lax.fori_loop(0, 16, whole, 0)

    def update(i, _):
        ys = row_y(i, r)
        local = same & (i == 0)

        @pl.when(local)
        def _():
            wait_bytes(grec.at[pl.ds(0, 3)], grs.at[ys])

        @pl.when(jnp.logical_not(local))
        def _():
            wait_bytes(grec.at[pl.ds(0, 4)], grs.at[ys])

        for n in range(4):
            s = ys * 4 + n
            rows = slot_rows(s)
            g = grec[s].astype(F32) * 0.25
            new_momentum = momentum_coef * mom[rows, :] + g
            mom[rows, :] = new_momentum
            mas[rows, :] = mas[rows, :] - outer_rate * (g + momentum_coef * new_momentum)
        rows = pl.ds(pl.multiple_of(ys * 4 * ROWS, ROWS), 4 * ROWS)
        pltpu.make_async_copy(mom.at[rows], out_momentum.at[rows], mosem).start()
        pltpu.make_async_copy(mas.at[rows], out_master.at[rows], masem).start()
        return 0

    lax.fori_loop(0, 4, update, 0)

    def pass_on(j, _):
        k = chunk(j)
        w_z(k).wait_recv()
        w_forward(k).start()
        w_keep(k).start()
        return 0

    lax.fori_loop(0, 16, pass_on, 0)

    wait_bytes(crec, css)
    wait_bytes(zbuf, zss)
    wait_bytes(zraw, xss)
    wait_bytes(rel, rss)
    for sem, buf, blocks, less in ((uss, ubuf, 8, same), (fss, ubuf, 8, passed), (gss, gbuf, 16, same)):

        @pl.when(less)
        def _():
            wait_bytes(buf.at[pl.ds(0, blocks - 1)], sem)

        @pl.when(jnp.logical_not(less))
        def _():
            wait_bytes(buf.at[pl.ds(0, blocks)], sem)

    wait_bytes(mom, mosem)
    wait_bytes(mas, masem)
    for sem in (wcs, wls, wcr, wzs, wms, wfs, wfr):
        wait_bytes(wbuf, sem)


def write_kernel(a, b, w, out_a, out_b, out_w, sems):
    copies = [
        pltpu.make_async_copy(a, out_a, sems.at[0]),
        pltpu.make_async_copy(b, out_b, sems.at[1]),
    ]
    copies += [
        pltpu.make_async_copy(w.at[pl.ds(i * 64, 64)], out_w.at[pl.ds(i * 64, 64)], sems.at[2 + i]) for i in range(4)
    ]
    for copy in copies:
        copy.start()
    for copy in copies:
        copy.wait()


def write(*results):
    free = pl.BlockSpec(memory_space=pl.ANY)
    return pl.pallas_call(
        write_kernel,
        out_shape=tuple(jax.ShapeDtypeStruct(a.shape, a.dtype) for a in results),
        in_specs=[free] * 3,
        out_specs=(free,) * 3,
        scratch_shapes=[pltpu.SemaphoreType.DMA((6,))],
        compiler_params=pltpu.CompilerParams(vmem_limit_bytes=1 * 2**20),
    )(*results)


def per_device(levels, scales, master, momentum):
    small = pltpu.VMEM((CHUNKS, ROWS, COLS), BF16)
    free = pl.BlockSpec(memory_space=pl.ANY)
    return write(*pl.pallas_call(
        kernel,
        out_shape=(
            jax.ShapeDtypeStruct(master.shape, F32),
            jax.ShapeDtypeStruct(momentum.shape, F32),
            jax.ShapeDtypeStruct(levels.shape[1:], BF16),
        ),
        in_specs=[pl.BlockSpec(memory_space=pltpu.HBM)] * 4,
        out_specs=(free,) * 3,
        scratch_shapes=[
            pltpu.VMEM((CHUNKS, 2 * ROWS, 2 * COLS), jnp.int32),
            pltpu.VMEM((64, 2 * ROWS), F32),
            pltpu.VMEM((2 * ROWS, 128), F32),
            pltpu.VMEM(master.shape, F32),
            pltpu.VMEM(momentum.shape, F32),
            pltpu.VMEM((2 * CHUNKS, 2 * ROWS, COLS), BF16),
            pltpu.VMEM((2 * CHUNKS, ROWS, COLS), BF16),
        ]
        + [small] * 6
        + [pltpu.VMEM((4, 2, ROWS, COLS), BF16)]
        + [small] * 2
        + [pltpu.VMEM((ROWS, HEAD), BF16)]
        + [pltpu.SemaphoreType.REGULAR] * 2
        + [pltpu.SemaphoreType.DMA((n,)) for n in (AHEAD, 18, 16, 16, 4, 4, 4, 16)],
        compiler_params=pltpu.CompilerParams(
            collective_id=0, has_side_effects=True, vmem_limit_bytes=40 * 2**20
        ),
    )(*[
        pltpu.with_memory_space_constraint(a, pltpu.HBM)
        for a in (levels, jnp.swapaxes(scales, 1, 2), master, momentum)
    ]))


def solution(mesh):
    in_specs = (
        P("replica", "fsdp", None),
        P("replica", "fsdp", None),
        P("replica", "fsdp"),
        P("replica", "fsdp"),
    )
    out_specs = (P("replica", "fsdp"), P("replica", "fsdp"), P("fsdp", None))
    return jax.shard_map(
        per_device, mesh=mesh, in_specs=in_specs, out_specs=out_specs, check_vma=False
    )
```

```python
import functools

import jax
import jax.numpy as jnp
from jax import lax
from jax.experimental import pallas as pl
from jax.experimental.pallas import tpu as pltpu
from jax.sharding import PartitionSpec as P

MESH = pl.DeviceIdType.MESH
F32 = jnp.float32
BF16 = jnp.bfloat16

BLOCK = 128
ROWS = 128
COLS = 256
CHUNKS = 16
HEAD = 128
TAIL = 128
AHEAD = 8
LAG = 2

outer_rate = 0.7
momentum_coef = 0.9
MOM = outer_rate * momentum_coef * momentum_coef
GRAD = outer_rate * (1.0 + momentum_coef)


def kernel(
    levels, scales, master, momentum,
    out_master, out_momentum, out_w,
    lv, sc, sc2, mas, mom, dec, crec, zbuf, zrec, gbuf, grec, ubuf, urec, rel, wbuf, wrec, zraw,
    near, far, lsem, one, crs, zrs, grs, urs, rrs, wzr,
):
    ssem, masem, mosem, css, zss, gss, uss, rss, fss, wzs, wcs, wcr, wfs, wfr, wls, wms, xss, xrs = (
        one.at[i] for i in range(18)
    )
    r = lax.axis_index("replica")
    f = lax.axis_index("fsdp")
    x, y, zh = f // 8, (f // 2) % 4, f % 2
    zl, c = r // 2, r % 2
    core = (zl * 2 + (1 - c), f)
    zp = ((1 - zl) * 2 + c, f)
    zd = ((1 - zl) * 2 + (1 - c), f)
    cross = (2 * (1 - zl) + c, x * 8 + y * 2 + 1 - zh)
    own = (zl + zh + x // 2) % 2
    same = r == x
    xf = 2 * (1 - zl) + c
    passed = xf == x
    my_slot = (y * 2 + zh) * 2 + c
    my_chunk = x * 4 + y
    herald = r == 0

    def chunk(j):
        b = j % 4
        return ((x + b) % 4) * 4 + (y + j // 4 + b) % 4

    def row_y(i, x_rows):
        return (y + 8 - (x + 4 - x_rows) % 4 - i) % 4

    bar = pltpu.get_barrier_semaphore()
    def load_scales():
        return pltpu.make_async_copy(scales.at[0], sc, ssem)

    def load_levels(j):
        cols = pl.ds(pl.multiple_of(chunk(j) * 2 * COLS, 2 * COLS), 2 * COLS)
        return pltpu.make_async_copy(levels.at[0, :, cols], lv.at[j], lsem.at[j % AHEAD])

    def load_master():
        return pltpu.make_async_copy(master, mas, masem)

    def load_momentum():
        return pltpu.make_async_copy(momentum, mom, mosem)

    load_scales().start()

    def load(j, _):
        load_levels(j).start()
        return 0

    load_levels(0).start()

    for member, greeted in ((0, (1, 2, 3)), (1, (2, 3)), (2, (1, 3)), (3, (1, 2))):

        @pl.when(r == member)
        def _():
            for other in greeted:
                pl.semaphore_signal(bar, inc=1, device_id=(other, f), device_id_type=MESH)

    lax.fori_loop(1, AHEAD, load, 0)
    load_master().start()
    load_momentum().start()

    load_scales().wait()
    by_row = jnp.transpose(sc[...])
    sc2[:, :64] = by_row
    sc2[:, 64:] = by_row

    def remote(src, dst, send, recv, device):
        return pltpu.make_async_remote_copy(
            src_ref=src, dst_ref=dst, send_sem=send, recv_sem=recv, device_id=device, device_id_type=MESH
        )

    def wait_bytes(like, sem):
        pltpu.make_async_copy(like, like, sem).wait()

    mine = pl.ds(pl.multiple_of(c * ROWS, ROWS), ROWS)
    others = pl.ds(pl.multiple_of((1 - c) * ROWS, ROWS), ROWS)

    def core_copy(k):
        return remote(dec.at[pl.ds(2 * k, 2), others, :], crec.at[pl.ds(2 * k, 2)], css, crs.at[k], core)

    def z_copy(k):
        return remote(zbuf.at[k], zrec.at[k], zss, zrs.at[k], zp)

    def head_copy(k):
        b = 2 * k + 1 - own
        return remote(dec.at[b, mine, pl.ds(0, HEAD)], zrec.at[k, :, pl.ds(0, HEAD)], zss, zrs.at[k], zp)

    def other_head_copy(k):
        return remote(dec.at[2 * k + 1 - own, others, pl.ds(0, HEAD)], zraw, xss, xrs, zd)

    def rest_copy(k):
        cols = pl.ds(HEAD, COLS - HEAD)
        return remote(zbuf.at[k, :, cols], zrec.at[k, :, cols], zss, zrs.at[k], zp)

    def u_copy(i):
        ys, cs = row_y(i // 2, r), (c + i) % 2
        s = (ys * 2 + zh) * 2 + cs
        return remote(ubuf.at[s], urec.at[my_chunk], uss, urs.at[i // 2], (2 * zl + cs, r * 8 + ys * 2 + zh))

    def relay_copy(i):
        ys = row_y(i, r)
        return remote(ubuf.at[pl.ds((ys * 2 + 1 - zh) * 2, 2)], rel.at[i], rss, rrs.at[i], cross)

    def forward_copy(i):
        ys, cs = row_y(i // 2, xf), (c + i) % 2
        return remote(
            rel.at[i // 2, cs], urec.at[my_chunk], fss, urs.at[i // 2], (2 * zl + cs, xf * 8 + ys * 2 + zh)
        )

    def g_copy(j):
        k = chunk(j)
        return remote(gbuf.at[k], grec.at[my_slot], gss, grs.at[y], (x, k * 2 + own))

    def columns(block):
        return pl.ds(pl.multiple_of(block * COLS, COLS), COLS)

    def w_z(k):
        return remote(wbuf.at[k], wrec.at[k], wzs, wzr.at[k], zp)

    def w_core(k):
        return remote(wbuf.at[k], out_w.at[mine, columns(2 * k + own)], wcs, wcr, core)

    def w_local(k):
        return pltpu.make_async_copy(wbuf.at[k], out_w.at[mine, columns(2 * k + own)], wls)

    def w_forward(k):
        return remote(wrec.at[k], out_w.at[mine, columns(2 * k + 1 - own)], wfs, wfr, core)

    def w_keep(k):
        return pltpu.make_async_copy(wrec.at[k], out_w.at[mine, columns(2 * k + 1 - own)], wms)

    def last_z(k):
        return remote(wbuf.at[k, :, pl.ds(0, TAIL)], wrec.at[k, :, pl.ds(0, TAIL)], wzs, wzr.at[k], zp)

    def tail_columns(block):
        return pl.ds(pl.multiple_of(block * COLS + TAIL, BLOCK), COLS - TAIL)

    def last_direct(k):
        cols = tail_columns(2 * k + own)
        return remote(wbuf.at[k, :, pl.ds(TAIL, COLS - TAIL)], out_w.at[mine, cols], wzs, wms, zp)

    def last_other(k):
        cols = tail_columns(2 * k + own)
        return remote(wbuf.at[k, :, pl.ds(TAIL, COLS - TAIL)], out_w.at[mine, cols], wfs, wfr, zd)

    def last_columns(k):
        return pl.ds(pl.multiple_of((2 * k + 1 - own) * COLS, COLS), TAIL)

    def last_forward(k):
        return remote(wrec.at[k, :, pl.ds(0, TAIL)], out_w.at[mine, last_columns(k)], wfs, wfr, core)

    def last_keep(k):
        return pltpu.make_async_copy(wrec.at[k, :, pl.ds(0, TAIL)], out_w.at[mine, last_columns(k)], wms)

    def slot_rows(s):
        return pl.ds(pl.multiple_of(s * ROWS, ROWS), ROWS)

    def send_z(j):
        k = chunk(j)
        b = 2 * k + 1 - own
        core_copy(k).wait_recv()
        zbuf[k] = (dec[b, mine, :].astype(F32) + crec[b].astype(F32)).astype(BF16)

        @pl.when(j == 0)
        def _():
            rest_copy(k).start()

        @pl.when(j > 0)
        def _():
            z_copy(k).start()

    def make_u(s):
        rows = slot_rows(s)
        ubuf[s] = (mas[rows, :] - MOM * mom[rows, :]).astype(BF16)

    def send_u(i, _):
        here = same & (i == 0)

        @pl.when(here)
        def _():
            urec[my_chunk] = ubuf[my_slot]

        @pl.when(jnp.logical_not(here))
        def _():
            u_copy(i).start()
        return 0

    def first(j, _):
        k = chunk(j)
        load_levels(j).wait()

        @pl.when(j < 16 - AHEAD)
        def _():
            load_levels(j + AHEAD).start()

        s = pltpu.roll(sc2[...], (128 - 4 * k) % 128, 1)
        for h in range(4):
            lanes = slice(h * BLOCK, (h + 1) * BLOCK)
            to = slice(h % 2 * BLOCK, (h % 2 + 1) * BLOCK)
            dec[2 * k + h // 2, :, to] = (lv[j, :, lanes].astype(F32) * s[:, h:h + 1]).astype(BF16)

        @pl.when((j == 0) & jnp.logical_not(herald))
        def _():
            pl.semaphore_wait(bar, 3)

        @pl.when((j == 0) & (r == 1))
        def _():
            pl.semaphore_signal(near, inc=1, device_id=(0, f), device_id_type=MESH)

        @pl.when((j == 0) & herald)
        def _():
            pl.semaphore_wait(near, 1)

        @pl.when(j == 0)
        def _():
            head_copy(k).start()
            other_head_copy(k).start()

        core_copy(k).start()

        @pl.when(j >= LAG)
        def _():
            send_z(j - LAG)

        @pl.when((j >= 1) & (j < 5))
        def _():
            for i in range(2):
                n = 8 * r + 2 * (j - 1) + i

                @pl.when(n > 0)
                def _():
                    pl.semaphore_signal(bar, inc=1, device_id=(0, (f + n) % 32), device_id_type=MESH)

        @pl.when(j == 3)
        def _():
            load_master().wait()
            load_momentum().wait()

        @pl.when((j >= 3) & (j < 3 + 4))
        def _():
            for i in range(4):
                make_u(4 * (j - 3) + i)

        @pl.when((j == 12) & herald)
        def _():
            pl.semaphore_wait(bar, 31)
            for member in (1, 2, 3):
                pl.semaphore_signal(far, inc=1, device_id=(member, f), device_id_type=MESH)

        @pl.when((j == 12) & jnp.logical_not(herald))
        def _():
            pl.semaphore_wait(far, 1)

        @pl.when(j == 12)
        def _():
            for i in range(4):
                relay_copy(i).start()
            lax.fori_loop(0, 8, send_u, 0)
        return 0

    lax.fori_loop(0, 16, first, 0)

    def drain(j, _):
        send_z(j)
        return 0

    lax.fori_loop(16 - LAG, 16, drain, 0)

    def send_forward(i, _):
        here = passed & (i == 0)

        @pl.when(i % 2 == 0)
        def _():
            relay_copy(i // 2).wait_recv()

        @pl.when(here)
        def _():
            urec[my_chunk] = rel[0, c]

        @pl.when(jnp.logical_not(here))
        def _():
            forward_copy(i).start()
        return 0

    lax.fori_loop(0, 8, send_forward, 0)

    def whole(j, _):
        k = chunk(j)
        b = 2 * k + own
        here = same & (j == 0)
        z_copy(k).wait_recv()

        @pl.when(j == 0)
        def _():
            other_head_copy(k).wait_recv()
            zrec[k, :, :HEAD] = (zrec[k, :, :HEAD].astype(F32) + zraw[...].astype(F32)).astype(BF16)

        gbuf[k] = (dec[b, mine, :].astype(F32) + crec[b].astype(F32) + zrec[k].astype(F32)).astype(BF16)

        @pl.when(here)
        def _():
            grec[my_slot] = gbuf[k]

        @pl.when(jnp.logical_not(here))
        def _():
            g_copy(j).start()

        local = (same | passed) & (j == 0)

        @pl.when(local)
        def _():
            wait_bytes(urec.at[pl.ds(0, 3)], urs.at[0])

        @pl.when((j % 4 == 0) & jnp.logical_not(local))
        def _():
            wait_bytes(urec.at[pl.ds(0, 4)], urs.at[j // 4])

        total = dec[b, mine, :].astype(F32) + crec[b].astype(F32) + zrec[k].astype(F32)
        wbuf[k] = (urec[k].astype(F32) - (GRAD / 4) * total).astype(BF16)

        @pl.when(j < 15)
        def _():
            w_z(k).start()

        @pl.when(j == 15)
        def _():
            last_z(k).start()
            last_direct(k).start()
            last_other(k).start()

        w_core(k).start()
        w_local(k).start()
        return 0

    lax.fori_loop(0, 16, whole, 0)

    def update(i, _):
        ys = row_y(i, r)
        local = same & (i == 0)

        @pl.when(local)
        def _():
            wait_bytes(grec.at[pl.ds(0, 3)], grs.at[ys])

        @pl.when(jnp.logical_not(local))
        def _():
            wait_bytes(grec.at[pl.ds(0, 4)], grs.at[ys])

        for n in range(4):
            s = ys * 4 + n
            rows = slot_rows(s)
            g = grec[s].astype(F32) * 0.25
            new_momentum = momentum_coef * mom[rows, :] + g
            mom[rows, :] = new_momentum
            mas[rows, :] = mas[rows, :] - outer_rate * (g + momentum_coef * new_momentum)
        rows = pl.ds(pl.multiple_of(ys * 4 * ROWS, ROWS), 4 * ROWS)
        pltpu.make_async_copy(mom.at[rows], out_momentum.at[rows], mosem).start()
        pltpu.make_async_copy(mas.at[rows], out_master.at[rows], masem).start()
        return 0

    lax.fori_loop(0, 4, update, 0)

    def pass_on(j, _):
        k = chunk(j)
        w_z(k).wait_recv()
        w_forward(k).start()
        w_keep(k).start()
        return 0

    lax.fori_loop(0, 15, pass_on, 0)
    last = chunk(15)
    last_z(last).wait_recv()
    last_forward(last).start()
    last_keep(last).start()

    wait_bytes(crec, css)
    wait_bytes(zbuf, zss)
    wait_bytes(zraw, xss)
    wait_bytes(rel, rss)
    for sem, buf, blocks, less in ((uss, ubuf, 8, same), (fss, ubuf, 8, passed), (gss, gbuf, 16, same)):

        @pl.when(less)
        def _():
            wait_bytes(buf.at[pl.ds(0, blocks - 1)], sem)

        @pl.when(jnp.logical_not(less))
        def _():
            wait_bytes(buf.at[pl.ds(0, blocks)], sem)

    wait_bytes(mom, mosem)
    wait_bytes(mas, masem)
    for sem in (wcs, wls, wcr, wzs, wms, wfs, wfr):
        wait_bytes(wbuf, sem)


def write_kernel(a, b, w, out_a, out_b, out_w, sems):
    copies = [
        pltpu.make_async_copy(a, out_a, sems.at[0]),
        pltpu.make_async_copy(b, out_b, sems.at[1]),
    ]
    copies += [
        pltpu.make_async_copy(w.at[pl.ds(i * 64, 64)], out_w.at[pl.ds(i * 64, 64)], sems.at[2 + i]) for i in range(4)
    ]
    for copy in copies:
        copy.start()
    for copy in copies:
        copy.wait()


def write(*results):
    free = pl.BlockSpec(memory_space=pl.ANY)
    return pl.pallas_call(
        write_kernel,
        out_shape=tuple(jax.ShapeDtypeStruct(a.shape, a.dtype) for a in results),
        in_specs=[free] * 3,
        out_specs=(free,) * 3,
        scratch_shapes=[pltpu.SemaphoreType.DMA((6,))],
        compiler_params=pltpu.CompilerParams(vmem_limit_bytes=1 * 2**20),
    )(*results)


def per_device(levels, scales, master, momentum):
    small = pltpu.VMEM((CHUNKS, ROWS, COLS), BF16)
    free = pl.BlockSpec(memory_space=pl.ANY)
    return write(*pl.pallas_call(
        kernel,
        out_shape=(
            jax.ShapeDtypeStruct(master.shape, F32),
            jax.ShapeDtypeStruct(momentum.shape, F32),
            jax.ShapeDtypeStruct(levels.shape[1:], BF16),
        ),
        in_specs=[pl.BlockSpec(memory_space=pltpu.HBM)] * 4,
        out_specs=(free,) * 3,
        scratch_shapes=[
            pltpu.VMEM((CHUNKS, 2 * ROWS, 2 * COLS), jnp.int32),
            pltpu.VMEM((64, 2 * ROWS), F32),
            pltpu.VMEM((2 * ROWS, 128), F32),
            pltpu.VMEM(master.shape, F32),
            pltpu.VMEM(momentum.shape, F32),
            pltpu.VMEM((2 * CHUNKS, 2 * ROWS, COLS), BF16),
            pltpu.VMEM((2 * CHUNKS, ROWS, COLS), BF16),
        ]
        + [small] * 6
        + [pltpu.VMEM((4, 2, ROWS, COLS), BF16)]
        + [small] * 2
        + [pltpu.VMEM((ROWS, HEAD), BF16)]
        + [pltpu.SemaphoreType.REGULAR] * 2
        + [pltpu.SemaphoreType.DMA((n,)) for n in (AHEAD, 18, 16, 16, 4, 4, 4, 16)],
        compiler_params=pltpu.CompilerParams(
            collective_id=0, has_side_effects=True, vmem_limit_bytes=40 * 2**20
        ),
    )(*[
        pltpu.with_memory_space_constraint(a, pltpu.HBM)
        for a in (levels, jnp.swapaxes(scales, 1, 2), master, momentum)
    ]))


def solution(mesh):
    in_specs = (
        P("replica", "fsdp", None),
        P("replica", "fsdp", None),
        P("replica", "fsdp"),
        P("replica", "fsdp"),
    )
    out_specs = (P("replica", "fsdp"), P("replica", "fsdp"), P("fsdp", None))
    return jax.shard_map(
        per_device, mesh=mesh, in_specs=in_specs, out_specs=out_specs, check_vma=False
    )
```
